32 devices in a mesh: path: 16 (over z, y, x), shard: 2 (over core).
Axes of the slice: x: 2, y: 2, z: 4, core: 2. Of those that a mesh axis runs over, the one named last changes fastest.
Arguments:
- features: bfloat16 [16, 512, 768], P('path', None, 'shard'), may hold values from -6 to 6
- path_weights: bfloat16 [16, 768, 3072], P('path', None, 'shard'), may hold values from -6 to 6
- cotangent: bfloat16 [16, 512, 3072], P('path', None, 'shard'), may hold values from -6 to 6
- path_module: int32 [16, 1], replicated, may hold values from 0 to 15
- outer_params: float32 [16, 768, 3072], P(None, 'path', 'shard'), may hold values from -6 to 6
- outer_moment: float32 [16, 768, 3072], P(None, 'path', 'shard'), may hold values from -2 to 2
Outputs:
- synced: bfloat16 [16, 768, 3072], P('path', None, 'shard')
- params_new: float32 [16, 768, 3072], P(None, 'path', 'shard')
- moment_new: float32 [16, 768, 3072], P(None, 'path', 'shard')
- grad_weight: bfloat16 [16, 768, 3072], P('path', None, 'shard')
- grad_input: bfloat16 [16, 512, 768], P('path', None, 'shard')
The draws below stay inside these ranges and needn't reach their ends.
Inputs may be any that keep to these rules, and one draw needn't show every extreme that they name: `path_module`: every module id is used by at least one path.
All inputs are finite; a program needn't handle non-finite values.
Results may differ from the reference program's by a relative error of at most 0.005.
Values may be sent and summed in bfloat16 or wider, within the bound.
A program may use at most 64 MiB of HBM per device.

```python
import jax
import jax.numpy as jnp
from jax import lax

D = 768
FF = 3072
MODULES = 16
TOK = 512
PATHS = 16


def level_of(key, dims, cuts, low, top_value):
    def one(axis_at, blocks):
        heights = jax.random.uniform(jax.random.fold_in(jax.random.fold_in(key, 6), axis_at), (blocks,), jnp.float32, low / len(cuts), top_value / len(cuts))
        return jnp.repeat(jnp.exp(heights), dims[axis_at] // blocks).reshape((-1,) + (1,) * (len(dims) - axis_at - 1))

    gain = one(*cuts[0])
    for cut in cuts[1:]:
        gain = gain * one(*cut)
    return gain


def choose_distinct(own_key, rows, amount, top, lift):
    sequence = jax.random.permutation(jax.random.fold_in(own_key, 1), amount)
    pull = sequence
    for power in range(3):
        pull = pull * pull // amount
    pull = pull * lift // amount
    lots = jax.random.randint(jax.random.fold_in(own_key, 2), (rows, amount), 0, 4096) + pull
    sure = jax.random.permutation(jax.random.fold_in(own_key, 3), rows)[jnp.arange(amount) % rows]
    lots = jnp.where(jnp.arange(rows)[:, None] == sure[None, :], 1 << 14, lots)
    merit = lots * amount + jnp.arange(amount)
    return lax.top_k(merit.astype(jnp.int32), top)[1].astype(jnp.int32)


def gaussian(own_key, extent, deviation, limit, split=(), kind=jnp.bfloat16):
    level = level_of(own_key, extent, split, -0.22, 0.18) if split else 1.0
    array = jax.random.normal(own_key, extent, jnp.float32) * deviation * level
    return jnp.minimum(jnp.maximum(array, -limit), limit).astype(kind)


def setup_inputs(seed: int = 0) -> dict:
    streams_of = jax.random.split(jax.random.key(seed), 7)
    features = gaussian(streams_of[0], (PATHS, TOK, D), 1.0, 6.0, ((0, 16), (2, 2)))
    path_weights = gaussian(streams_of[1], (PATHS, D, FF), 1.0, 6.0, ((0, 16), (2, 2)))
    cotangent = gaussian(streams_of[2], (PATHS, TOK, FF), 1.0, 6.0, ((0, 16), (2, 2)))
    path_module = choose_distinct(streams_of[3], PATHS, MODULES, 1, 512)
    outer_params = gaussian(streams_of[4], (MODULES, D, FF), 1.0, 6.0, ((1, 16), (2, 2)), jnp.float32)
    outer_moment = gaussian(streams_of[5], (MODULES, D, FF), 0.3, 2.0, ((1, 16), (2, 2)), jnp.float32)
    return dict(features=features, path_weights=path_weights, cotangent=cotangent, path_module=path_module, outer_params=outer_params, outer_moment=outer_moment)


outer_momentum = 0.9
outer_rate = 0.7


def silu_slope(pre):
    sigmoid_part = jax.nn.sigmoid(pre)
    return sigmoid_part * (1.0 + pre * (1.0 - sigmoid_part))


def reference(features, path_weights, cotangent, path_module, outer_params, outer_moment):
    multiplier = D ** -0.5

    def inner_layer(operands):
        tokens_in, weights_in, upstream = operands
        pre = jnp.dot(tokens_in, weights_in, preferred_element_type=jnp.float32) * multiplier
        delta = (upstream.astype(jnp.float32) * silu_slope(pre)).astype(jnp.bfloat16)
        grad_w = (jnp.dot(tokens_in.T, delta, preferred_element_type=jnp.float32) * multiplier).astype(jnp.bfloat16)
        grad_in = (jnp.dot(delta, weights_in.T, preferred_element_type=jnp.float32) * multiplier).astype(jnp.bfloat16)
        return grad_w, grad_in

    grad_weight, grad_input = lax.map(inner_layer, (features, path_weights, cotangent))
    modules = path_module[:, 0].astype(jnp.int32)

    def add_path(totals, operands):
        module_id, weights_in = operands
        return totals.at[module_id].add(weights_in.astype(jnp.float32)), None

    totals, unused = lax.scan(add_path, jnp.zeros((MODULES, D, FF), jnp.float32), (modules, path_weights))
    member = (modules[None, :] == jnp.arange(MODULES, dtype=jnp.int32)[:, None]).astype(jnp.float32)
    counts = jnp.sum(member, axis=1)
    average = totals / counts[:, None, None]
    pseudo = outer_params - average
    moment_new = outer_momentum * outer_moment + pseudo
    params_new = outer_params - outer_rate * (pseudo + outer_momentum * moment_new)
    rounded = params_new.astype(jnp.bfloat16)
    synced = rounded[modules]
    return synced, params_new, moment_new, grad_weight, grad_input
```

```python
import functools

import jax
import jax.numpy as jnp
from jax import lax
from jax.experimental import pallas as pl
from jax.experimental.pallas import tpu as pltpu
from jax.sharding import PartitionSpec as P

outer_momentum = 0.9
outer_rate = 0.7


def silu_slope(pre):
    sigmoid_part = jax.nn.sigmoid(pre)
    return sigmoid_part * (1.0 + pre * (1.0 - sigmoid_part))


def partner(index, count, flips):
    result = 0
    place = 1
    while place < count:
        bit = lax.rem(lax.div(index, place), 2)
        result = result + place * (1 - bit if flips & place else bit)
        place *= 2
    return result


def send_order(count):
    return sorted(range(1, count), key=lambda flips: (flips < count // 2, flips))


def fused_kernel(
    count,
    module_ref,
    features_hbm,
    weights_hbm,
    cotangent_hbm,
    params_hbm,
    moment_hbm,
    synced_ref,
    params_new_ref,
    moment_new_ref,
    grad_weight_ref,
    grad_input_ref,
    tokens,
    weights,
    cotangent,
    params,
    moment,
    received,
    own,
    returned,
    terms,
    terms_other,
    local_sem,
    out_send,
    out_recv,
    back_send,
    back_recv,
    pair_send,
    pair_recv,
):
    me = lax.axis_index("path")
    core = lax.axis_index("shard")
    other = 1 - core
    rows, columns = params.shape[1:]
    depth = count * rows
    order = send_order(count)

    def block_of(path):
        return pl.ds(pl.multiple_of(path * rows, rows), rows)

    local = [
        pltpu.make_async_copy(params_hbm, params, local_sem.at[0]),
        pltpu.make_async_copy(moment_hbm, moment, local_sem.at[1]),
        pltpu.make_async_copy(weights_hbm, weights, local_sem.at[2]),
        pltpu.make_async_copy(cotangent_hbm, cotangent, local_sem.at[3]),
        pltpu.make_async_copy(features_hbm, tokens.at[core], local_sem.at[4]),
        pltpu.make_async_copy(weights_hbm.at[block_of(me)], received.at[me], local_sem.at[5]),
    ]
    for copy in local:
        copy.start()

    barrier = pltpu.get_barrier_semaphore()
    for flips in order:
        pl.semaphore_signal(barrier, inc=1, device_id={"path": partner(me, count, flips)})
    pl.semaphore_signal(barrier, inc=1, device_id={"shard": other})
    pl.semaphore_wait(barrier, count)

    outward = []
    for flips in order:
        peer = partner(me, count, flips)
        copy = pltpu.make_async_remote_copy(
            src_ref=weights_hbm.at[block_of(peer)],
            dst_ref=received.at[me],
            send_sem=out_send.at[flips],
            recv_sem=out_recv.at[flips],
            device_id={"path": peer},
        )
        copy.start()
        outward.append(copy)
    give_tokens = pltpu.make_async_remote_copy(
        src_ref=features_hbm,
        dst_ref=tokens.at[core],
        send_sem=pair_send.at[0],
        recv_sem=pair_recv.at[0],
        device_id={"shard": other},
    )
    give_tokens.start()

    local[0].wait()
    local[1].wait()

    def own_block(path):
        at = module_ref[path]
        shaped = params[at]
        moved = outer_momentum * moment[at] + shaped
        return shaped - outer_rate * (shaped + outer_momentum * moved)

    @pl.loop(0, count)
    def _(path):
        own[path] = own_block(path).astype(own.dtype)

    back = []
    for flips in order:
        peer = partner(me, count, flips)
        copy = pltpu.make_async_remote_copy(
            src_ref=own.at[peer],
            dst_ref=returned.at[me],
            send_sem=back_send.at[flips],
            recv_sem=back_recv.at[flips],
            device_id={"path": peer},
        )
        copy.start()
        back.append(copy)

    share = outer_rate * (1.0 + outer_momentum)
    for copy in local[2:]:
        copy.wait()
    synced_ref[block_of(me), :] = (
        own_block(me) + share * weights[block_of(me), :].astype(jnp.float32)
    ).astype(synced_ref.dtype)
    give_tokens.wait()

    multiplier = depth ** (-0.5)
    half = depth // 2
    tile = 256
    terms[...] = jnp.zeros_like(terms)

    @pl.loop(0, columns // tile)
    def _(step):
        cols = pl.ds(pl.multiple_of(step * tile, tile), tile)
        pre = jnp.dot(tokens[0], weights[:half, cols], preferred_element_type=jnp.float32)
        pre += jnp.dot(tokens[1], weights[half:, cols], preferred_element_type=jnp.float32)
        slope = silu_slope(pre * multiplier)
        delta = (cotangent[:, cols].astype(jnp.float32) * slope).astype(jnp.bfloat16)
        for part in range(2):
            grad = lax.dot_general(
                tokens[part], delta, (((0,), (0,)), ((), ())), preferred_element_type=jnp.float32
            )
            grad_weight_ref[part * half : (part + 1) * half, cols] = (grad * multiplier).astype(
                grad_weight_ref.dtype
            )
            terms[part] += lax.dot_general(
                delta,
                weights[part * half : (part + 1) * half, cols],
                (((1,), (1,)), ((), ())),
                preferred_element_type=jnp.float32,
            )

    give_terms = pltpu.make_async_remote_copy(
        src_ref=terms.at[other],
        dst_ref=terms_other,
        send_sem=pair_send.at[1],
        recv_sem=pair_recv.at[1],
        device_id={"shard": other},
    )
    give_terms.start()
    give_terms.wait()
    grad_input_ref[...] = ((terms[core] + terms_other[...]) * multiplier).astype(
        grad_input_ref.dtype
    )

    for copy in outward:
        copy.wait()

    @pl.loop(0, count)
    def _(at):
        path = lax.fori_loop(
            0, count, lambda i, found: jnp.where(module_ref[i] == at, i, found), jnp.int32(0)
        )
        shaped = params[at]
        pseudo = shaped - received[path].astype(jnp.float32)
        moved = outer_momentum * moment[at] + pseudo
        moment_new_ref[at] = moved
        params_new_ref[at] = shaped - outer_rate * (pseudo + outer_momentum * moved)

    for flips, copy in zip(order, back):
        copy.wait()
        peer = partner(me, count, flips)
        synced_ref[block_of(peer), :] = (
            returned[peer].astype(jnp.float32)
            + share * weights[block_of(peer), :].astype(jnp.float32)
        ).astype(synced_ref.dtype)


def fused(features, weights_here, cotangent, path_module, outer_params, outer_moment):
    count, rows, columns = outer_params.shape
    depth = weights_here.shape[0]
    tokens, half = features.shape
    anywhere = pl.BlockSpec(memory_space=pl.ANY)
    sixteen = jnp.bfloat16
    return pl.pallas_call(
        functools.partial(fused_kernel, count),
        in_specs=[pl.BlockSpec(memory_space=pltpu.SMEM)] + [anywhere] * 5,
        out_specs=[pl.BlockSpec(memory_space=pltpu.VMEM)] * 5,
        out_shape=[
            pltpu.VMEM((depth, columns), sixteen),
            pltpu.VMEM(outer_params.shape, jnp.float32),
            pltpu.VMEM(outer_params.shape, jnp.float32),
            pltpu.VMEM((depth, columns), sixteen),
            pltpu.VMEM((tokens, half), sixteen),
        ],
        scratch_shapes=[
            pltpu.VMEM((2, tokens, half), sixteen),
            pltpu.VMEM((depth, columns), sixteen),
            pltpu.VMEM((tokens, columns), sixteen),
            pltpu.VMEM(outer_params.shape, jnp.float32),
            pltpu.VMEM(outer_params.shape, jnp.float32),
            pltpu.VMEM(outer_params.shape, sixteen),
            pltpu.VMEM(outer_params.shape, sixteen),
            pltpu.VMEM(outer_params.shape, sixteen),
            pltpu.VMEM((2, tokens, half), jnp.float32),
            pltpu.VMEM((tokens, half), jnp.float32),
            pltpu.SemaphoreType.DMA((6,)),
            pltpu.SemaphoreType.DMA((count,)),
            pltpu.SemaphoreType.DMA((count,)),
            pltpu.SemaphoreType.DMA((count,)),
            pltpu.SemaphoreType.DMA((count,)),
            pltpu.SemaphoreType.DMA((2,)),
            pltpu.SemaphoreType.DMA((2,)),
        ],
        compiler_params=pltpu.CompilerParams(
            collective_id=0, has_side_effects=True, vmem_limit_bytes=40 * 2**20
        ),
    )(path_module[:, 0], features, weights_here, cotangent, outer_params, outer_moment)


def many_paths_each(weights_here, path_module, outer_params, outer_moment):
    count_path = lax.axis_size("path")
    module_count = outer_params.shape[0]
    received = lax.all_to_all(weights_here, "path", split_axis=0, concat_axis=0, tiled=True)
    flattened = received.reshape(count_path, -1)
    modules = path_module[:, 0]
    member = modules[None, :] == jnp.arange(module_count, dtype=jnp.int32)[:, None]
    summed = jnp.dot(member.astype(jnp.bfloat16), flattened, preferred_element_type=jnp.float32)
    counts = jnp.sum(member.astype(jnp.float32), axis=1)
    average = summed / counts[:, None]
    shaped = outer_params.reshape(module_count, -1)
    pseudo = shaped - average
    moment_flat = outer_momentum * outer_moment.reshape(module_count, -1) + pseudo
    params_flat = shaped - outer_rate * (pseudo + outer_momentum * moment_flat)
    chosen = jnp.dot(
        member.T.astype(jnp.bfloat16),
        params_flat.astype(jnp.bfloat16),
        preferred_element_type=jnp.float32,
    )
    chosen = chosen.astype(jnp.bfloat16).reshape(received.shape)
    returned = lax.all_to_all(chosen, "path", split_axis=0, concat_axis=0, tiled=True)
    return returned, params_flat.reshape(outer_params.shape), moment_flat.reshape(outer_moment.shape)


def inner_layer(features, weights_here, cotangent):
    tokens_full = lax.all_gather(features, "shard", axis=1, tiled=True)
    multiplier = tokens_full.shape[1] ** (-0.5)
    pre = jnp.dot(tokens_full, weights_here, preferred_element_type=jnp.float32) * multiplier
    delta = (cotangent.astype(jnp.float32) * silu_slope(pre)).astype(jnp.bfloat16)
    grad_w = lax.dot_general(
        tokens_full, delta, (((0,), (0,)), ((), ())), preferred_element_type=jnp.float32
    )
    grad_w = (grad_w * multiplier).astype(jnp.bfloat16)
    terms = lax.dot_general(
        delta, weights_here, (((1,), (1,)), ((), ())), preferred_element_type=jnp.float32
    )
    terms = terms * multiplier
    whole = lax.psum(terms, "shard")
    width = terms.shape[1] // lax.axis_size("shard")
    grad_in = lax.dynamic_slice_in_dim(whole, lax.axis_index("shard") * width, width, 1)
    return grad_w, grad_in.astype(jnp.bfloat16)


def fits_fused(weights_here, outer_params):
    count, rows, columns = outer_params.shape
    return (
        lax.axis_size("path") == count
        and count & (count - 1) == 0
        and lax.axis_size("shard") == 2
        and rows % 16 == 0
        and columns % 256 == 0
        and (count * rows) % 256 == 0
    )


def on_device(features, path_weights, cotangent, path_module, outer_params, outer_moment):
    weights_here = path_weights[0]
    if fits_fused(weights_here, outer_params):
        synced, params_new, moment_new, grad_weight, grad_input = fused(
            features[0], weights_here, cotangent[0], path_module, outer_params, outer_moment
        )
    else:
        synced, params_new, moment_new = many_paths_each(
            weights_here, path_module, outer_params, outer_moment
        )
        grad_weight, grad_input = inner_layer(features[0], weights_here, cotangent[0])
    return (synced[None], params_new, moment_new, grad_weight[None], grad_input[None])


def solution(mesh):
    return jax.shard_map(
        on_device,
        mesh=mesh,
        in_specs=(
            P("path", None, "shard"),
            P("path", None, "shard"),
            P("path", None, "shard"),
            P(),
            P(None, "path", "shard"),
            P(None, "path", "shard"),
        ),
        out_specs=(
            P("path", None, "shard"),
            P(None, "path", "shard"),
            P(None, "path", "shard"),
            P("path", None, "shard"),
            P("path", None, "shard"),
        ),
        check_vma=False,
    )
```

```python
import functools

import jax
import jax.numpy as jnp
from jax import lax
from jax.experimental import pallas as pl
from jax.experimental.pallas import tpu as pltpu
from jax.sharding import PartitionSpec as P

outer_momentum = 0.9
outer_rate = 0.7


def silu_slope(pre):
    sigmoid_part = jax.nn.sigmoid(pre)
    return sigmoid_part * (1.0 + pre * (1.0 - sigmoid_part))


def partner(index, count, flips):
    result = 0
    place = 1
    while place < count:
        bit = lax.rem(lax.div(index, place), 2)
        flip = lax.rem(lax.div(flips, place), 2)
        result = result + place * (bit + flip - 2 * bit * flip)
        place *= 2
    return result


def send_plan(count):
    far = range(count // 2, count)
    near = range(1, count // 2)
    order = [k for pair in zip(far, near) for k in pair] + [count - 1]
    return [(kind, k, k) for kind in ("out", "back") for k in order]


def fused_kernel(
    count,
    module_hbm,
    features_hbm,
    weights_hbm,
    cotangent_hbm,
    params_hbm,
    moment_hbm,
    synced_ref,
    params_new_ref,
    moment_new_ref,
    grad_weight_ref,
    grad_input_ref,
    module_ref,
    tokens,
    weights,
    cotangent,
    params,
    moment,
    received,
    own,
    returned,
    terms,
    terms_other,
    local_sem,
    out_send,
    out_recv,
    back_send,
    back_recv,
    pair_send,
    pair_recv,
):
    me = lax.axis_index("path")
    core = lax.axis_index("shard")
    other = 1 - core
    rows, columns = params.shape[1:]
    depth = count * rows
    plan = send_plan(count)

    def block_of(path):
        return pl.ds(pl.multiple_of(path * rows, rows), rows)

    local = [
        pltpu.make_async_copy(module_hbm, module_ref, local_sem.at[6]),
        pltpu.make_async_copy(params_hbm, params, local_sem.at[0]),
        pltpu.make_async_copy(moment_hbm, moment, local_sem.at[1]),
        pltpu.make_async_copy(weights_hbm, weights, local_sem.at[2]),
        pltpu.make_async_copy(cotangent_hbm, cotangent, local_sem.at[3]),
        pltpu.make_async_copy(features_hbm, tokens.at[core], local_sem.at[4]),
        pltpu.make_async_copy(weights_hbm.at[block_of(me)], received.at[me], local_sem.at[5]),
    ]
    barrier = pltpu.get_barrier_semaphore()
    for flips in range(1, count):
        peer = partner(me, count, jnp.int32(flips))
        pl.semaphore_signal(barrier, inc=1, device_id={"path": peer})
    pl.semaphore_signal(barrier, inc=1, device_id={"shard": other})
    pl.semaphore_wait(barrier, count)

    give_tokens = pltpu.make_async_remote_copy(
        src_ref=features_hbm,
        dst_ref=tokens.at[core],
        send_sem=pair_send.at[0],
        recv_sem=pair_recv.at[0],
        device_id={"shard": other},
    )

    def own_block(path):
        at = module_ref[0, path]
        shaped = params[at]
        moved = outer_momentum * moment[at] + shaped
        return shaped - outer_rate * (shaped + outer_momentum * moved)

    outward, back = [], []
    for exchange, first, second in plan:
        flips = first + core * jnp.int32(second - first)
        peer = partner(me, count, flips)
        if exchange == "out":
            copy = pltpu.make_async_remote_copy(
                src_ref=weights_hbm.at[block_of(peer)],
                dst_ref=received.at[me],
                send_sem=out_send.at[len(outward)],
                recv_sem=out_recv.at[len(outward)],
                device_id={"path": peer},
            )
            copy.start()
            outward.append(copy)
            continue
        if not back:
            for copy in local:
                copy.start()
            give_tokens.start()
            for copy in local[:3]:
                copy.wait()

            @pl.loop(0, count)
            def _(path):
                own[path] = own_block(path).astype(own.dtype)

        copy = pltpu.make_async_remote_copy(
            src_ref=own.at[peer],
            dst_ref=returned.at[me],
            send_sem=back_send.at[len(back)],
            recv_sem=back_recv.at[len(back)],
            device_id={"path": peer},
        )
        copy.start()
        back.append((peer, copy))

    share = outer_rate * (1.0 + outer_momentum)
    for copy in local[3:]:
        copy.wait()
    synced_ref[block_of(me), :] = (
        own_block(me) + share * weights[block_of(me), :].astype(jnp.float32)
    ).astype(synced_ref.dtype)
    give_tokens.wait()

    multiplier = depth ** (-0.5)
    half = depth // 2
    tile = 256
    terms[...] = jnp.zeros_like(terms)

    @pl.loop(0, columns // tile)
    def _(step):
        cols = pl.ds(pl.multiple_of(step * tile, tile), tile)
        pre = jnp.dot(tokens[0], weights[:half, cols], preferred_element_type=jnp.float32)
        pre += jnp.dot(tokens[1], weights[half:, cols], preferred_element_type=jnp.float32)
        slope = silu_slope(pre * multiplier)
        delta = (cotangent[:, cols].astype(jnp.float32) * slope).astype(jnp.bfloat16)
        for part in range(2):
            grad = lax.dot_general(
                tokens[part], delta, (((0,), (0,)), ((), ())), preferred_element_type=jnp.float32
            )
            grad_weight_ref[part * half : (part + 1) * half, cols] = (grad * multiplier).astype(
                grad_weight_ref.dtype
            )
            terms[part] += lax.dot_general(
                delta,
                weights[part * half : (part + 1) * half, cols],
                (((1,), (1,)), ((), ())),
                preferred_element_type=jnp.float32,
            )

    give_terms = pltpu.make_async_remote_copy(
        src_ref=terms.at[other],
        dst_ref=terms_other,
        send_sem=pair_send.at[1],
        recv_sem=pair_recv.at[1],
        device_id={"shard": other},
    )
    give_terms.start()
    give_terms.wait()
    grad_input_ref[...] = ((terms[core] + terms_other[...]) * multiplier).astype(
        grad_input_ref.dtype
    )

    for copy in outward:
        copy.wait()

    @pl.loop(0, count)
    def _(at):
        path = lax.fori_loop(
            0, count, lambda i, found: jnp.where(module_ref[0, i] == at, i, found), jnp.int32(0)
        )
        shaped = params[at]
        pseudo = shaped - received[path].astype(jnp.float32)
        moved = outer_momentum * moment[at] + pseudo
        moment_new_ref[at] = moved
        params_new_ref[at] = shaped - outer_rate * (pseudo + outer_momentum * moved)

    for peer, copy in back:
        copy.wait()
        synced_ref[block_of(peer), :] = (
            returned[peer].astype(jnp.float32)
            + share * weights[block_of(peer), :].astype(jnp.float32)
        ).astype(synced_ref.dtype)


def write_kernel(*refs):
    sources, targets, sem = refs[:5], refs[5:10], refs[10]
    copies = [
        pltpu.make_async_copy(source, target, sem.at[i])
        for i, (source, target) in enumerate(zip(sources, targets))
    ]
    for copy in copies:
        copy.start()
    for copy in copies:
        copy.wait()


def write(*arrays):
    anywhere = pl.BlockSpec(memory_space=pl.ANY)
    return pl.pallas_call(
        write_kernel,
        in_specs=[anywhere] * 5,
        out_specs=[anywhere] * 5,
        out_shape=[jax.ShapeDtypeStruct(array.shape, array.dtype) for array in arrays],
        scratch_shapes=[pltpu.SemaphoreType.DMA((5,))],
        compiler_params=pltpu.CompilerParams(vmem_limit_bytes=2**20),
    )(*arrays)


def fused(features, weights_here, cotangent, path_module, outer_params, outer_moment):
    count, rows, columns = outer_params.shape
    depth = weights_here.shape[0]
    tokens, half = features.shape
    anywhere = pl.BlockSpec(memory_space=pl.ANY)
    sixteen = jnp.bfloat16
    results = pl.pallas_call(
        functools.partial(fused_kernel, count),
        in_specs=[anywhere] * 6,
        out_specs=[pl.BlockSpec(memory_space=pltpu.VMEM)] * 5,
        out_shape=[
            pltpu.VMEM((depth, columns), sixteen),
            pltpu.VMEM(outer_params.shape, jnp.float32),
            pltpu.VMEM(outer_params.shape, jnp.float32),
            pltpu.VMEM((depth, columns), sixteen),
            pltpu.VMEM((tokens, half), sixteen),
        ],
        scratch_shapes=[
            pltpu.SMEM((1, count), jnp.int32),
            pltpu.VMEM((2, tokens, half), sixteen),
            pltpu.VMEM((depth, columns), sixteen),
            pltpu.VMEM((tokens, columns), sixteen),
            pltpu.VMEM(outer_params.shape, jnp.float32),
            pltpu.VMEM(outer_params.shape, jnp.float32),
            pltpu.VMEM(outer_params.shape, sixteen),
            pltpu.VMEM(outer_params.shape, sixteen),
            pltpu.VMEM(outer_params.shape, sixteen),
            pltpu.VMEM((2, tokens, half), jnp.float32),
            pltpu.VMEM((tokens, half), jnp.float32),
            pltpu.SemaphoreType.DMA((7,)),
            pltpu.SemaphoreType.DMA((count,)),
            pltpu.SemaphoreType.DMA((count,)),
            pltpu.SemaphoreType.DMA((count,)),
            pltpu.SemaphoreType.DMA((count,)),
            pltpu.SemaphoreType.DMA((2,)),
            pltpu.SemaphoreType.DMA((2,)),
        ],
        compiler_params=pltpu.CompilerParams(
            collective_id=0, has_side_effects=True, vmem_limit_bytes=40 * 2**20
        ),
    )(path_module.reshape(1, count), features, weights_here, cotangent, outer_params, outer_moment)
    return write(*[pltpu.with_memory_space_constraint(x, pltpu.VMEM) for x in results])


def many_paths_each(weights_here, path_module, outer_params, outer_moment):
    count_path = lax.axis_size("path")
    module_count = outer_params.shape[0]
    received = lax.all_to_all(weights_here, "path", split_axis=0, concat_axis=0, tiled=True)
    flattened = received.reshape(count_path, -1)
    modules = path_module[:, 0]
    member = modules[None, :] == jnp.arange(module_count, dtype=jnp.int32)[:, None]
    summed = jnp.dot(member.astype(jnp.bfloat16), flattened, preferred_element_type=jnp.float32)
    counts = jnp.sum(member.astype(jnp.float32), axis=1)
    average = summed / counts[:, None]
    shaped = outer_params.reshape(module_count, -1)
    pseudo = shaped - average
    moment_flat = outer_momentum * outer_moment.reshape(module_count, -1) + pseudo
    params_flat = shaped - outer_rate * (pseudo + outer_momentum * moment_flat)
    chosen = jnp.dot(
        member.T.astype(jnp.bfloat16),
        params_flat.astype(jnp.bfloat16),
        preferred_element_type=jnp.float32,
    )
    chosen = chosen.astype(jnp.bfloat16).reshape(received.shape)
    returned = lax.all_to_all(chosen, "path", split_axis=0, concat_axis=0, tiled=True)
    return returned, params_flat.reshape(outer_params.shape), moment_flat.reshape(outer_moment.shape)


def inner_layer(features, weights_here, cotangent):
    tokens_full = lax.all_gather(features, "shard", axis=1, tiled=True)
    multiplier = tokens_full.shape[1] ** (-0.5)
    pre = jnp.dot(tokens_full, weights_here, preferred_element_type=jnp.float32) * multiplier
    delta = (cotangent.astype(jnp.float32) * silu_slope(pre)).astype(jnp.bfloat16)
    grad_w = lax.dot_general(
        tokens_full, delta, (((0,), (0,)), ((), ())), preferred_element_type=jnp.float32
    )
    grad_w = (grad_w * multiplier).astype(jnp.bfloat16)
    terms = lax.dot_general(
        delta, weights_here, (((1,), (1,)), ((), ())), preferred_element_type=jnp.float32
    )
    terms = terms * multiplier
    whole = lax.psum(terms, "shard")
    width = terms.shape[1] // lax.axis_size("shard")
    grad_in = lax.dynamic_slice_in_dim(whole, lax.axis_index("shard") * width, width, 1)
    return grad_w, grad_in.astype(jnp.bfloat16)


def fits_fused(weights_here, outer_params):
    count, rows, columns = outer_params.shape
    return (
        lax.axis_size("path") == count
        and count & (count - 1) == 0
        and lax.axis_size("shard") == 2
        and rows % 16 == 0
        and columns % 256 == 0
        and (count * rows) % 256 == 0
    )


def on_device(features, path_weights, cotangent, path_module, outer_params, outer_moment):
    weights_here = path_weights[0]
    if fits_fused(weights_here, outer_params):
        synced, params_new, moment_new, grad_weight, grad_input = fused(
            features[0], weights_here, cotangent[0], path_module, outer_params, outer_moment
        )
    else:
        synced, params_new, moment_new = many_paths_each(
            weights_here, path_module, outer_params, outer_moment
        )
        grad_weight, grad_input = inner_layer(features[0], weights_here, cotangent[0])
    return (synced[None], params_new, moment_new, grad_weight[None], grad_input[None])


def solution(mesh):
    return jax.shard_map(
        on_device,
        mesh=mesh,
        in_specs=(
            P("path", None, "shard"),
            P("path", None, "shard"),
            P("path", None, "shard"),
            P(),
            P(None, "path", "shard"),
            P(None, "path", "shard"),
        ),
        out_specs=(
            P("path", None, "shard"),
            P(None, "path", "shard"),
            P(None, "path", "shard"),
            P("path", None, "shard"),
            P("path", None, "shard"),
        ),
        check_vma=False,
    )
```
